32 devices in a mesh: groups: 2 (over y), blk: 4 (over z), draw: 2 (over x), sub: 2 (over core).
Axes of the slice: x: 2, y: 2, z: 4, core: 2. Of those that a mesh axis runs over, the one named last changes fastest.
Arguments:
- white_noise: float32 [4, 32, 128, 128], P(None, ('groups', 'blk', 'sub'), 'draw'), parts along dimension 1, may hold values from -6 to 6
- coupling: bfloat16 [4, 32, 6, 128, 128], P(None, ('groups', 'blk', 'sub')), parts along dimension 1, may hold values from -0.21875 to 0.21875
- diag_inv: bfloat16 [4, 32, 128, 128], P(None, ('groups', 'blk', 'sub')), parts along dimension 1, may hold values from -0.5 to 0.5
- prior_far: bfloat16 [32, 128, 128], P(('groups', 'blk', 'sub'), 'draw'), parts along dimension 0, may hold values from -6 to 6
- prior_near: bfloat16 [32, 128, 128], P(('groups', 'blk', 'sub'), 'draw'), parts along dimension 0, may hold values from -6 to 6
- neighbours: int32 [4, 32, 6], P(None, ('groups', 'blk', 'sub')), parts along dimension 1, may hold values from 0 to 15, as said below
- spot_map: int32 [16384], P(('groups', 'blk', 'sub')), parts along dimension 0, may hold values from 0 to 8191, as said below
Outputs:
- posterior_draws: bfloat16 [128, 16384], P('draw', ('groups', 'blk', 'sub')), parts along dimension 1
The draws below stay inside these ranges and needn't reach their ends.
There are 2 independent parts, one for each index of `groups`. The reference program is written for one: setup_inputs(seed, part) draws one part's arguments, and reference() takes and returns one part's arrays. A program takes and returns all parts, laid end to end along the dimension named above; each array names one. Nothing has to cross between parts.
Inputs may be any that keep to these rules, and one draw needn't show every extreme that they name: Entries index blocks of one level; an owner holds the aligned runs of 2 blocks of each level. For every owner of reading blocks, every level of solved blocks and every owner of those blocks, at most 2 distinct blocks of that owner are read by the reading owner's blocks of the two levels that read that level, and this most is reached in every draw; the neighbours of one block are distinct. `spot_map`: A permutation of 0 .. 8191. Every aligned run of 1024 entries (one owner's points) places exactly 128 points in every spatial shard, a shard being an aligned run of 1024 positions.
All inputs are finite; a program needn't handle non-finite values.
Results may differ from the reference program's by a relative error of at most 0.0063.
Values may be sent and summed in bfloat16 or wider, within the bound.
A program may use at most 64 MiB of HBM per device.

```python
import jax
import jax.numpy as jnp

BS = 128
DRAWS = 128
K1 = 4
K2 = 2
LEVELS = 4
LB = 2
OWNERS = 8
BLOCKS = 16
PTS_DEV = 1024
NWIN = 8192
PER_PAIR = 128


def draw_neighbours(key, part):
    key = jax.random.fold_in(key, 11)
    sections = LEVELS + 1
    count = LB * (K1 + K2)
    key_perm, key_base = jax.random.split(key)
    perm_keys = jax.random.split(key_perm, sections * OWNERS)
    orders = jax.vmap(lambda subkey: jax.random.permutation(subkey, OWNERS))(perm_keys)
    orders = orders.reshape(sections, OWNERS, OWNERS)
    offsets = jax.random.randint(key_base, (sections, OWNERS, OWNERS), 0, LB)
    read_idx = jnp.arange(count)
    owner_ids = orders[:, :, read_idx % OWNERS]
    step_idx = read_idx // OWNERS
    base_slot = jnp.take_along_axis(offsets, owner_ids, axis=2)
    slot_idx = (base_slot + step_idx[None, None, :]) % LB
    listing = owner_ids * LB + slot_idx
    fresh_part = listing[1:, :, :LB * K1].reshape(LEVELS, OWNERS, LB, K1)
    older_part = listing[:-1, :, LB * K1:].reshape(LEVELS, OWNERS, LB, K2)
    joined = jnp.concatenate([fresh_part, older_part], axis=-1)
    return joined.reshape(LEVELS, OWNERS * LB, K1 + K2).astype(jnp.int32)


def draw_spot_map(key, part):
    key = jax.random.fold_in(key, 23)
    key_dest, key_src = jax.random.split(key)
    dest_orders = jax.vmap(lambda subkey: jax.random.permutation(subkey, PTS_DEV))(jax.random.split(key_dest, OWNERS))
    places = jnp.arange(OWNERS)[:, None] * PTS_DEV + dest_orders
    places = places.reshape(OWNERS, OWNERS, PER_PAIR).transpose(1, 0, 2).reshape(OWNERS, PTS_DEV)
    src_orders = jax.vmap(lambda subkey: jax.random.permutation(subkey, PTS_DEV))(jax.random.split(key_src, OWNERS))
    shuffled = jnp.take_along_axis(places, src_orders, axis=1)
    return shuffled.reshape(OWNERS * PTS_DEV).astype(jnp.int32)


def level_of(rng, dims, shards, least, top_value):
    factor_of = 1.0
    for axis_at, shards_of in shards:
        steps = jax.random.uniform(jax.random.fold_in(jax.random.fold_in(rng, 6), axis_at), (shards_of,), jnp.float32, least / len(shards), top_value / len(shards))
        factor_of = factor_of * jnp.repeat(jnp.exp(steps), dims[axis_at] // shards_of).reshape((-1,) + (1,) * (len(dims) - 1 - axis_at))
    return factor_of


def gaussian(stream_key, dims, spread, limit, shards=(), dtype=jnp.bfloat16):
    gain = level_of(stream_key, dims, shards, -0.22, 0.18) if shards else 1.0
    array = jax.random.normal(stream_key, dims, jnp.float32) * spread * gain
    return jnp.minimum(jnp.maximum(array, -limit), limit).astype(dtype)


def setup_inputs(seed: int = 0, part: int = 0) -> dict:
    keys = jax.random.split(jax.random.key(seed), 8)
    part_keys = jax.random.split(jax.random.fold_in(keys[7], part), 8)
    return {
        "white_noise": gaussian(part_keys[0], (LEVELS, BLOCKS, DRAWS, BS), 1.0, 6.0, ((1, 8), (2, 2)), jnp.float32),
        "coupling": gaussian(part_keys[1], (LEVELS, BLOCKS, K1 + K2, BS, BS), ((K1 + K2) * BS) ** -0.5, 0.21875, ((1, 8),)),
        "diag_inv": gaussian(part_keys[2], (LEVELS, BLOCKS, BS, BS), BS ** -0.5, 0.5, ((1, 8),)),
        "prior_far": gaussian(part_keys[3], (BLOCKS, DRAWS, BS), 1.0, 6.0, ((0, 8), (1, 2))),
        "prior_near": gaussian(part_keys[4], (BLOCKS, DRAWS, BS), 1.0, 6.0, ((0, 8), (1, 2))),
        "neighbours": draw_neighbours(jax.random.fold_in(jax.random.fold_in(keys[7], part), 71), part),
        "spot_map": draw_spot_map(jax.random.fold_in(jax.random.fold_in(keys[7], part), 71), part),
    }


def reference(white_noise, coupling, diag_inv, prior_far, prior_near, neighbours, spot_map):
    older_pool = prior_far
    newer_pool = prior_near
    levels = []
    for level_idx in range(LEVELS):
        neighbour_ids = neighbours[level_idx]
        fresh_rows = jnp.take(newer_pool, neighbour_ids[:, :K1], axis=0)
        older_rows = jnp.take(older_pool, neighbour_ids[:, K1:], axis=0)
        gathered = jnp.concatenate([fresh_rows, older_rows], axis=1)
        carried = jnp.einsum("bkfp,bkpq->bfq", gathered.astype(jnp.float32), coupling[level_idx].astype(jnp.float32))
        remain = (white_noise[level_idx] - carried).astype(jnp.bfloat16)
        solved = jnp.einsum("bfp,bpq->bfq", remain.astype(jnp.float32), diag_inv[level_idx].astype(jnp.float32))
        solved = solved.astype(jnp.bfloat16)
        levels.append(solved)
        older_pool = newer_pool
        newer_pool = solved
    stacked = jnp.stack(levels)
    flattened = stacked.reshape(LEVELS, OWNERS, LB, DRAWS, BS).transpose(3, 1, 0, 2, 4).reshape(DRAWS, NWIN)
    return jnp.zeros_like(flattened).at[:, spot_map].set(flattened)
```

```python
import functools

import jax
import jax.numpy as jnp
from jax import lax
from jax.experimental import pallas as pl
from jax.experimental.pallas import tpu as pltpu
from jax.sharding import PartitionSpec as P

K1 = 4
HALVES = 2
LANES = 128
OWN = ("blk", "sub")
MESH = pl.DeviceIdType.MESH
F32 = jnp.float32
BF16 = jnp.bfloat16


def repeat(count, body):
    if count <= 8:
        for at in range(count):
            body(at)
    else:
        pl.loop(0, count)(body)


def sweep(
    dims, regroup, neigh, spots, white_hbm, coup_hbm, diag_hbm, far, near, out,
    white, coup, diag, pool, flat, place, unplace, moved, landed, pos_out, pos_in, total,
    load_sem, own_sem, send_sem, hop_sem, recv_sem, pos_send, pos_recv, move_send, move_recv,
):
    blks, subs, levels, lb, draws, neighs = dims
    owners = blks * subs
    z, c = lax.axis_index("blk"), lax.axis_index("sub")
    me = z * subs + c
    half = draws // HALVES

    def device(owner):
        return {"blk": owner // subs, "sub": lax.rem(owner, subs)}

    def peer(step):
        return lax.rem(me + step, owners)

    def ahead(step):
        return lax.rem(z + step, blks)

    mates = subs - 1

    loads = [
        pltpu.make_async_copy(src, dst, load_sem.at[i])
        for i, (src, dst) in enumerate(((coup_hbm, coup), (white_hbm, white), (diag_hbm, diag)))
    ]
    for load in loads:
        load.start()

    def mine(sec, h):
        return pool[sec][h].at[pl.ds(me * lb, lb)]

    def section_of(sec, h):
        if sec < 2:
            ref = (far, near)[sec]
            return ref.at[:, pl.ds(h * half, half), :]
        return mine(sec, h)

    def own_copy(sec, h):
        return pltpu.make_async_copy(section_of(sec, h), mine(sec, h), own_sem.at[sec, h])

    def along(sec, h, step):
        return pltpu.make_async_remote_copy(
            section_of(sec, h), mine(sec, h), send_sem.at[sec, h, step], recv_sem.at[sec, h, me],
            device_id={"blk": ahead(step), "sub": c}, device_id_type=MESH)

    def across(sec, h):
        return pltpu.make_async_remote_copy(
            section_of(sec, h), mine(sec, h), send_sem.at[sec, h, 0], recv_sem.at[sec, h, me],
            device_id={"sub": mates - c}, device_id_type=MESH)

    def relay(sec, h, step):
        owner = lax.rem(z + blks - step, blks) * subs + c
        slot = pool[sec][h].at[pl.ds(owner * lb, lb)]
        return pltpu.make_async_remote_copy(
            slot, slot, hop_sem.at[sec, h, step], recv_sem.at[sec, h, owner],
            device_id={"sub": mates - c}, device_id_type=MESH)

    def arrival(sec, h, owner):
        slot = pool[sec][h].at[pl.ds(owner * lb, lb)]
        return pltpu.make_async_remote_copy(
            slot, slot, hop_sem.at[sec, h, 0], recv_sem.at[sec, h, owner],
            device_id={"sub": mates - c}, device_id_type=MESH)

    def share(sec, h):
        repeat(blks - 1, lambda i: along(sec, h, i + 1).start())
        across(sec, h).start()

    def collect(secs, h):
        for sec in secs:
            def pass_on(i, sec=sec):
                owner = lax.rem(z + blks - (i + 1), blks) * subs + c
                arrival(sec, h, owner).wait_recv()
                relay(sec, h, i + 1).start()
            repeat(blks - 1, pass_on)
        for sec in secs:
            def take(i, sec=sec):
                owner = lax.rem(z + blks - i, blks) * subs + mates - c
                arrival(sec, h, owner).wait_recv()
            repeat(blks, take)

    barrier = pltpu.get_barrier_semaphore()
    repeat(owners - 1, lambda i: pl.semaphore_signal(
        barrier, inc=1, device_id=device(peer(i + 1)), device_id_type=MESH))
    for h in range(HALVES):
        for sec in (1, 0):
            own_copy(sec, h).start()
    pl.semaphore_wait(barrier, owners - 1)
    for h in range(HALVES):
        for sec in (1, 0):
            share(sec, h)

    chunks = levels * lb
    points = chunks * LANES
    place_of = lambda: lax.broadcasted_iota(jnp.int32, (LANES, points), 1).astype(F32)

    def pos_copy(step):
        to = peer(step)
        return pltpu.make_async_remote_copy(
            pos_out.at[to], pos_in.at[me], pos_send.at[step], pos_recv.at[me],
            device_id=device(to), device_id_type=MESH)

    def pos_arrival(owner):
        return pltpu.make_async_remote_copy(
            pos_out.at[owner], pos_in.at[owner], pos_send.at[0], pos_recv.at[owner],
            device_id=device(peer(1)), device_id_type=MESH)

    def move_copy(step):
        to = peer(step)
        return pltpu.make_async_remote_copy(
            moved.at[to], landed.at[me], move_send.at[step], move_recv.at[me],
            device_id=device(to), device_id_type=MESH)

    def move_arrival(owner):
        return pltpu.make_async_remote_copy(
            moved.at[owner], landed.at[owner], move_send.at[0], move_recv.at[owner],
            device_id=device(peer(1)), device_id_type=MESH)

    def rank_points():
        spot = spots[...]
        rows = spot.astype(F32)
        cols = rows.T
        local = lax.rem(spot, points).astype(F32).T
        lane = place_of()
        ordered = jnp.zeros((1, points), F32)
        for k in range(chunks):
            col = cols[:, k:k + 1]
            below = jnp.zeros((LANES, LANES), F32)
            for j in range(chunks):
                below += jnp.where(rows[j:j + 1, :] < col, 1.0, 0.0)
            rank = jnp.sum(below, axis=1, keepdims=True)
            hit = lane == rank
            place[k * LANES:(k + 1) * LANES, :] = jnp.where(hit, 1.0, 0.0).astype(BF16)
            ordered += jnp.sum(jnp.where(hit, local[:, k:k + 1], 0.0), axis=0, keepdims=True)
        for s in range(owners):
            pos_out[s] = jnp.broadcast_to(ordered[:, s * LANES:(s + 1) * LANES], (8, LANES))
        for i in range(1, owners):
            pos_copy(i).start()
        pos_in[me] = pos_out[me]

    def place_arrivals():
        lane = place_of()
        for i in range(1, owners):
            pos_arrival(peer(i)).wait_recv()
        for o in range(owners):
            col = pos_in[o].T[:, 0:1]
            unplace[o * LANES:(o + 1) * LANES, :] = jnp.where(lane == col, 1.0, 0.0).astype(BF16)

    if regroup:
        rank_points()

    for h in range(HALVES):
        for sec in (1, 0):
            own_copy(sec, h).wait()
    for load in loads:
        load.wait()

    def tiles(level, b, h, sec, first, last):
        rows = jnp.concatenate([pool[sec][h][neigh[level, b, k]] for k in range(first, last)], axis=1)
        factor = coup[level, b, first:last].reshape((last - first) * LANES, LANES)
        return jnp.dot(rows, factor, preferred_element_type=F32)

    for level in range(levels):
        for h in range(HALVES):
            if level == 0:
                collect((1, 0), h)
            rest = [
                white[level, b, h * half:(h + 1) * half, :] - tiles(level, b, h, level, K1, neighs)
                for b in range(lb)
            ]
            if level > 0:
                collect((level + 1,), h)
            for b in range(lb):
                remain = (rest[b] - tiles(level, b, h, level + 1, 0, K1)).astype(BF16)
                solved = jnp.dot(remain, diag[level, b], preferred_element_type=F32).astype(BF16)
                flat[level * lb + b, h * half:(h + 1) * half, :] = solved
                if level + 1 < levels:
                    pool[level + 2][h][me * lb + b] = solved
            if level + 1 < levels:
                share(level + 2, h)
        if regroup:
            part = sum(
                jnp.dot(flat[k], place[k * LANES:(k + 1) * LANES, :], preferred_element_type=F32)
                for k in range(level * lb, (level + 1) * lb)
            )
            if level == 0:
                total[...] = part
                place_arrivals()
            elif level + 1 < levels:
                total[...] += part
            else:
                final = (total[...] + part).astype(BF16)
                for s in range(owners):
                    moved[s] = final[:, s * LANES:(s + 1) * LANES]
                for i in range(1, owners):
                    move_copy(i).start()

    if regroup:
        def laid(ref, o):
            return jnp.dot(ref[o], unplace[pl.ds(pl.multiple_of(o * LANES, LANES), LANES), :],
                           preferred_element_type=F32)

        total[...] = laid(moved, me)
        for i in range(1, owners):
            owner = peer(i)
            move_arrival(owner).wait_recv()
            total[...] += laid(landed, owner)
        out[...] = total[...].astype(BF16)
        for i in range(1, owners):
            pos_copy(i).wait_send()
            move_copy(i).wait_send()
    else:
        out[...] = flat[...]
    for sec in range(levels + 1):
        for h in range(HALVES):
            def sent(i, sec=sec, h=h):
                along(sec, h, i + 1).wait_send()
                relay(sec, h, i + 1).wait_send()
            repeat(blks - 1, sent)
            across(sec, h).wait_send()


def shards(white_noise, coupling, diag_inv, prior_far, prior_near, neighbours, spot_map):
    blks, subs = lax.axis_size("blk"), lax.axis_size("sub")
    owners = blks * subs
    levels, lb, draws, size = white_noise.shape
    points = spot_map.shape[0]
    per_pair = points // owners
    regroup = per_pair == LANES
    chunks = levels * lb
    secs = levels + 1
    dims = (blks, subs, levels, lb, draws, neighbours.shape[2])
    out_shape = (draws, points) if regroup else (chunks, draws, size)
    dma = pltpu.SemaphoreType.DMA
    vmem, smem = pl.BlockSpec(memory_space=pltpu.VMEM), pl.BlockSpec(memory_space=pltpu.SMEM)
    anywhere = pl.BlockSpec(memory_space=pl.ANY)
    pairs = owners if regroup else 1
    flops = 2 * draws * size * size * chunks * 7 + 4 * draws * points * points
    result = pl.pallas_call(
        functools.partial(sweep, dims, regroup),
        out_shape=jax.ShapeDtypeStruct(out_shape, BF16),
        in_specs=[smem, vmem] + [anywhere] * 5,
        out_specs=vmem,
        scratch_shapes=[
            pltpu.VMEM(white_noise.shape, F32),
            pltpu.VMEM(coupling.shape, BF16),
            pltpu.VMEM(diag_inv.shape, BF16),
            [[pltpu.VMEM((owners * lb, draws // HALVES, size), BF16)] * HALVES] * secs,
            pltpu.VMEM((chunks, draws, size), BF16),
            pltpu.VMEM((points, points), BF16),
            pltpu.VMEM((points, points), BF16),
            pltpu.VMEM((pairs, draws, LANES), BF16),
            pltpu.VMEM((pairs, draws, LANES), BF16),
            pltpu.VMEM((pairs, 8, LANES), F32),
            pltpu.VMEM((pairs, 8, LANES), F32),
            pltpu.VMEM((draws, points), F32),
            dma((3,)),
            dma((2, HALVES)),
            dma((secs, HALVES, blks)),
            dma((secs, HALVES, blks)),
            dma((secs, HALVES, owners)),
            dma((owners,)),
            dma((owners,)),
            dma((owners,)),
            dma((owners,)),
        ],
        compiler_params=pltpu.CompilerParams(
            collective_id=0, has_side_effects=True, vmem_limit_bytes=48 * 1024 * 1024),
        cost_estimate=pl.CostEstimate(flops=flops, bytes_accessed=3 * 2**20, transcendentals=0),
    )(neighbours, spot_map.reshape(points // LANES, LANES), white_noise, coupling, diag_inv,
      prior_far, prior_near)
    if regroup:
        return result
    ordering = jnp.argsort(spot_map)
    sorted_spots = jnp.take(spot_map, ordering).reshape(owners, per_pair)
    placings = lax.all_to_all(sorted_spots, OWN, split_axis=0, concat_axis=0, tiled=True)
    local = result.transpose(1, 0, 2).reshape(draws, points)
    moving = jnp.take(local, ordering, axis=1).reshape(draws, owners, per_pair)
    arrived = lax.all_to_all(moving, OWN, split_axis=1, concat_axis=1, tiled=True)
    spot_local = placings.reshape(-1) % points
    return jnp.zeros((draws, points), BF16).at[:, spot_local].set(arrived.reshape(draws, points))


def solution(mesh):
    return jax.shard_map(
        shards,
        mesh=mesh,
        in_specs=(
            P(None, ("groups", "blk", "sub"), "draw", None),
            P(None, ("groups", "blk", "sub"), None, None, None),
            P(None, ("groups", "blk", "sub"), None, None),
            P(("groups", "blk", "sub"), "draw", None),
            P(("groups", "blk", "sub"), "draw", None),
            P(None, ("groups", "blk", "sub"), None),
            P(("groups", "blk", "sub")),
        ),
        out_specs=P("draw", ("groups", "blk", "sub")),
        check_vma=False,
    )
```

```python
import functools

import jax
import jax.numpy as jnp
from jax import lax
from jax.experimental import pallas as pl
from jax.experimental.pallas import tpu as pltpu
from jax.sharding import PartitionSpec as P

K1 = 4
HALVES = 2
LANES = 128
OWN = ("blk", "sub")
MESH = pl.DeviceIdType.MESH
F32 = jnp.float32
BF16 = jnp.bfloat16


def repeat(count, body):
    if count <= 8:
        for at in range(count):
            body(at)
    else:
        pl.loop(0, count)(body)


def sweep(
    dims, regroup, neigh_hbm, spots_hbm, white_hbm, coup_hbm, diag_hbm, far, near, out,
    neigh, neigh_vm, spots, white, coup, diag, pool, flat, place, unplace, moved, landed,
    pos_out, pos_in, total, load_sem, push_send, push_recv, smem_sem, own_sem, prior_send,
    prior_recv, level_send, level_recv, pos_send, pos_recv, move_send, move_recv, stay_sem,
):
    blks, subs, levels, lb, draws, neighs = dims
    owners = blks * subs
    z, c = lax.axis_index("blk"), lax.axis_index("sub")
    me = z * subs + c
    mate = subs - 1 - c
    share_of = draws // subs
    half = share_of // HALVES
    chunks = levels * lb
    points = spots.shape[1] * LANES

    def device(owner):
        return {"blk": owner // subs, "sub": lax.rem(owner, subs)}

    def peer(step):
        return lax.rem(me + step, owners)

    def chip(step):
        return lax.rem(z + step, blks)

    def rows_of(core):
        return pl.ds(pl.multiple_of(core * share_of, share_of), share_of)

    wares = [(spots_hbm, spots.at[c]), (neigh_hbm, neigh_vm.at[c])]
    wares += [(coup_hbm.at[0], coup.at[c, 0]), (diag_hbm, diag.at[c])]
    wares += [(coup_hbm.at[i], coup.at[c, i]) for i in range(1, levels)]
    noise_at = len(wares)

    def load(i):
        src, dst = wares[i]
        return pltpu.make_async_copy(src, dst, load_sem.at[i])

    def push(i):
        src, dst = wares[i]
        return pltpu.make_async_remote_copy(
            src, dst, push_send.at[i], push_recv.at[i], device_id={"sub": mate}, device_id_type=MESH)

    def load_noise():
        return pltpu.make_async_copy(
            white_hbm.at[:, :, rows_of(c), :], white.at[c], load_sem.at[noise_at])

    def push_noise():
        return pltpu.make_async_remote_copy(
            white_hbm.at[:, :, rows_of(mate), :], white.at[c], push_send.at[noise_at],
            push_recv.at[noise_at], device_id={"sub": mate}, device_id_type=MESH)

    def ready(i):
        load(i).wait()
        push(i).wait_recv()

    priors = (far, near)

    def prior_rows(sec, h, core):
        return priors[sec].at[:, pl.ds(pl.multiple_of(core * share_of + h * half, half), half), :]

    def prior_slot(sec, h, owner):
        return pool[sec][h].at[pl.ds(owner * lb, lb)]

    def prior_stay(sec, h):
        return pltpu.make_async_copy(prior_rows(sec, h, c), prior_slot(sec, h, me), own_sem.at[sec, h])

    def prior_copy(sec, h, step, core):
        return pltpu.make_async_remote_copy(
            prior_rows(sec, h, core), prior_slot(sec, h, me), prior_send.at[sec, h, step, core],
            prior_recv.at[sec, h, me], device_id={"blk": chip(step), "sub": core}, device_id_type=MESH)

    def prior_across(sec, h):
        return pltpu.make_async_remote_copy(
            prior_rows(sec, h, mate), prior_slot(sec, h, me), prior_send.at[sec, h, 0, 0],
            prior_recv.at[sec, h, me], device_id={"sub": mate}, device_id_type=MESH)

    def prior_arrival(sec, h, owner):
        slot = prior_slot(sec, h, owner)
        return pltpu.make_async_remote_copy(
            slot, slot, prior_send.at[sec, h, 0, 0], prior_recv.at[sec, h, owner],
            device_id={"sub": mate}, device_id_type=MESH)

    def share_prior(sec, h):
        for core in range(subs):
            repeat(blks - 1, lambda i, core=core: prior_copy(sec, h, i + 1, core).start())
        prior_across(sec, h).start()

    def level_slot(sec, h, at):
        return pool[sec][h].at[pl.ds(at * (subs * lb), subs * lb)]

    def level_copy(sec, h, step):
        return pltpu.make_async_remote_copy(
            level_slot(sec, h, z), level_slot(sec, h, z), level_send.at[sec - 2, h, step],
            level_recv.at[sec - 2, h, z], device_id={"blk": chip(step), "sub": c}, device_id_type=MESH)

    def level_arrival(sec, h, at):
        return pltpu.make_async_remote_copy(
            level_slot(sec, h, at), level_slot(sec, h, at), level_send.at[sec - 2, h, 0],
            level_recv.at[sec - 2, h, at], device_id={"blk": chip(1), "sub": c}, device_id_type=MESH)

    def collect(sec, h):
        if sec < 2:
            prior_stay(sec, h).wait()
            repeat(owners - 1, lambda i: prior_arrival(sec, h, peer(i + 1)).wait_recv())
        else:
            repeat(blks - 1, lambda i: level_arrival(sec, h, chip(i + 1)).wait_recv())

    def pos_copy(step):
        to = peer(step)
        return pltpu.make_async_remote_copy(
            pos_out.at[to], pos_in.at[me], pos_send.at[step], pos_recv.at[me],
            device_id=device(to), device_id_type=MESH)

    def pos_arrival(owner):
        return pltpu.make_async_remote_copy(
            pos_out.at[owner], pos_in.at[owner], pos_send.at[0], pos_recv.at[owner],
            device_id=device(peer(1)), device_id_type=MESH)

    def landing(at, core):
        return landed.at[pl.ds(at * subs, subs), rows_of(core), :]

    def move_copy(step):
        to = peer(step)
        return pltpu.make_async_remote_copy(
            moved.at[to], landing(z, c), move_send.at[step], move_recv.at[me],
            device_id=device(to), device_id_type=MESH)

    def move_stay():
        return pltpu.make_async_copy(moved.at[me], landing(z, c), stay_sem.at[0])

    def move_arrival(at, core):
        owner = at * subs + core
        return pltpu.make_async_remote_copy(
            moved.at[owner], landing(at, core), move_send.at[0], move_recv.at[owner],
            device_id=device(peer(1)), device_id_type=MESH)

    def lane():
        return lax.broadcasted_iota(jnp.int32, (LANES, points), 1).astype(F32)

    def rank_points(owner, own):
        spot = spots[owner]
        rows = spot.astype(F32)
        cols = rows.T
        local = lax.rem(spot, points).astype(F32).T
        ordered = jnp.zeros((1, points), F32)
        for k in range(chunks):
            col = cols[:, k:k + 1]
            below = jnp.zeros((LANES, LANES), F32)
            for j in range(chunks):
                below += jnp.where(rows[j:j + 1, :] < col, 1.0, 0.0)
            rank = jnp.sum(below, axis=1, keepdims=True)
            hit = lane() == rank
            place[owner, k * LANES:(k + 1) * LANES, :] = jnp.where(hit, 1.0, 0.0).astype(BF16)
            if own:
                ordered += jnp.sum(jnp.where(hit, local[:, k:k + 1], 0.0), axis=0, keepdims=True)
        if own:
            for s in range(owners):
                pos_out[s] = jnp.broadcast_to(ordered[:, s * LANES:(s + 1) * LANES], (8, LANES))
            pos_in[me] = pos_out[me]

    def place_arrivals():
        for i in range(1, owners):
            pos_arrival(peer(i)).wait_recv()
        for o in range(owners):
            col = pos_in[o].T[:, 0:1]
            unplace[o * LANES:(o + 1) * LANES, :] = jnp.where(lane() == col, 1.0, 0.0).astype(BF16)

    barrier = pltpu.get_barrier_semaphore()
    repeat(owners - 1, lambda i: pl.semaphore_signal(
        barrier, inc=1, device_id=device(peer(i + 1)), device_id_type=MESH))
    for i in range(2):
        load(i).start()
    for h in range(HALVES):
        for sec in (1, 0):
            prior_stay(sec, h).start()
    for i in range(2, noise_at):
        load(i).start()
    load_noise().start()
    load(0).wait()
    if regroup:
        rank_points(c, True)
    pl.semaphore_wait(barrier, owners - 1)
    for sec in (1, 0):
        share_prior(sec, 0)
    for i in range(4):
        push(i).start()
    push_noise().start()
    for h in range(1, HALVES):
        for sec in (1, 0):
            share_prior(sec, h)
    for i in range(4, noise_at):
        push(i).start()
    if regroup:
        for i in range(1, owners):
            pos_copy(i).start()
    push(0).wait_recv()
    if regroup:
        rank_points(mate, False)
    ready(1)
    to_smem = pltpu.make_async_copy(neigh_vm, neigh, smem_sem.at[0])
    to_smem.start()
    to_smem.wait()
    load_noise().wait()
    push_noise().wait_recv()
    for i in (2, 3):
        ready(i)

    def tiles(level, o, b, h, sec, first, last):
        rows = jnp.concatenate([pool[sec][h][neigh[o, level, b, k]] for k in range(first, last)], axis=1)
        factor = coup[o, level, b, first:last].reshape((last - first) * LANES, LANES)
        return jnp.dot(rows, factor, preferred_element_type=F32)

    blocks = [(o, b) for o in range(subs) for b in range(lb)]
    for level in range(levels):
        if level > 0:
            ready(level + 3)
        for h in range(HALVES):
            span = slice(h * half, (h + 1) * half)
            if level == 0:
                collect(0, h)
            rest = [
                white[o, level, b, span, :] - tiles(level, o, b, h, level, K1, neighs)
                for o, b in blocks
            ]
            collect(level + 1, h)
            remain = [
                (r - tiles(level, o, b, h, level + 1, 0, K1)).astype(BF16)
                for r, (o, b) in zip(rest, blocks)
            ]
            for r, (o, b) in zip(remain, blocks):
                solved = jnp.dot(r, diag[o, level, b], preferred_element_type=F32).astype(BF16)
                flat[o, level * lb + b, span, :] = solved
                if level + 1 < levels:
                    pool[level + 2][h][z * (subs * lb) + o * lb + b] = solved
            if level + 1 < levels:
                repeat(blks - 1, lambda i: level_copy(level + 2, h, i + 1).start())
        if regroup:
            for o in range(subs):
                part = sum(
                    jnp.dot(flat[o, k], place[o, k * LANES:(k + 1) * LANES, :], preferred_element_type=F32)
                    for k in range(level * lb, (level + 1) * lb)
                )
                if level == 0:
                    total[o] = part
                elif level + 1 < levels:
                    total[o] += part
                else:
                    final = (total[o] + part).astype(BF16)
                    for s in range(owners):
                        moved[s, o] = final[:, s * LANES:(s + 1) * LANES]
            if level == 0:
                place_arrivals()

    if regroup:
        for i in range(1, owners):
            move_copy(i).start()
        move_stay().start()

        def laid(at):
            rows = jnp.concatenate([landed[at * subs + o] for o in range(subs)], axis=1)
            width = subs * LANES
            return jnp.dot(rows, unplace[pl.ds(pl.multiple_of(at * width, width), width), :],
                           preferred_element_type=F32)

        move_stay().wait()
        move_arrival(z, mate).wait_recv()
        whole = laid(z)
        for i in range(1, blks):
            for core in range(subs):
                move_arrival(chip(i), core).wait_recv()
            whole += laid(chip(i))
        out[...] = whole.astype(BF16)
        for i in range(1, owners):
            pos_copy(i).wait_send()
            move_copy(i).wait_send()
    else:
        out[...] = flat[...]
    for h in range(HALVES):
        for sec in range(2):
            for core in range(subs):
                repeat(blks - 1, lambda i: prior_copy(sec, h, i + 1, core).wait_send())
            prior_across(sec, h).wait_send()
        for sec in range(2, levels + 1):
            repeat(blks - 1, lambda i: level_copy(sec, h, i + 1).wait_send())
    for i in range(noise_at):
        push(i).wait_send()
    push_noise().wait_send()


def shards(white_noise, coupling, diag_inv, prior_far, prior_near, neighbours, spot_map):
    blks, subs = lax.axis_size("blk"), lax.axis_size("sub")
    owners = blks * subs
    levels, lb, draws, size = white_noise.shape
    points = spot_map.shape[0]
    per_pair = points // owners
    regroup = per_pair == LANES
    chunks = levels * lb
    secs = levels + 1
    dims = (blks, subs, levels, lb, draws, neighbours.shape[2])
    share_of = draws // subs
    half = share_of // HALVES
    out_shape = (draws, points) if regroup else (subs, chunks, share_of, size)
    dma = pltpu.SemaphoreType.DMA
    vmem = pl.BlockSpec(memory_space=pltpu.VMEM)
    hbm = pl.BlockSpec(memory_space=pltpu.HBM)
    pairs = owners if regroup else 1
    flops = 2 * draws * size * size * chunks * 7 + 4 * draws * points * points
    result = pl.pallas_call(
        functools.partial(sweep, dims, regroup),
        out_shape=jax.ShapeDtypeStruct(out_shape, BF16),
        in_specs=[hbm] * 7,
        out_specs=vmem,
        scratch_shapes=[
            pltpu.SMEM((subs, *neighbours.shape), jnp.int32),
            pltpu.VMEM((subs, *neighbours.shape), jnp.int32),
            pltpu.VMEM((subs, points // LANES, LANES), jnp.int32),
            pltpu.VMEM((subs, levels, lb, share_of, size), F32),
            pltpu.VMEM((subs, *coupling.shape), BF16),
            pltpu.VMEM((subs, *diag_inv.shape), BF16),
            [[pltpu.VMEM((owners * lb, half, size), BF16)] * HALVES] * secs,
            pltpu.VMEM((subs, chunks, share_of, size), BF16),
            pltpu.VMEM((subs, points, points), BF16),
            pltpu.VMEM((points, points), BF16),
            pltpu.VMEM((pairs, subs, share_of, LANES), BF16),
            pltpu.VMEM((pairs, draws, LANES), BF16),
            pltpu.VMEM((pairs, 8, LANES), F32),
            pltpu.VMEM((pairs, 8, LANES), F32),
            pltpu.VMEM((subs, share_of, points), F32),
            dma((levels + 4,)),
            dma((levels + 4,)),
            dma((levels + 4,)),
            dma((1,)),
            dma((2, HALVES)),
            dma((2, HALVES, blks, subs)),
            dma((2, HALVES, owners)),
            dma((levels - 1, HALVES, blks)),
            dma((levels - 1, HALVES, blks)),
            dma((owners,)),
            dma((owners,)),
            dma((owners,)),
            dma((owners,)),
            dma((1,)),
        ],
        compiler_params=pltpu.CompilerParams(
            collective_id=0, has_side_effects=True, vmem_limit_bytes=60 * 1024 * 1024),
        cost_estimate=pl.CostEstimate(flops=flops, bytes_accessed=3 * 2**20, transcendentals=0),
    )(neighbours, spot_map.reshape(points // LANES, LANES), white_noise, coupling, diag_inv,
      prior_far, prior_near)
    if regroup:
        return result
    ordering = jnp.argsort(spot_map)
    sorted_spots = jnp.take(spot_map, ordering).reshape(owners, per_pair)
    placings = lax.all_to_all(sorted_spots, OWN, split_axis=0, concat_axis=0, tiled=True)
    result = lax.all_to_all(result, "sub", split_axis=0, concat_axis=2, tiled=True)[0]
    local = result.transpose(1, 0, 2).reshape(draws, points)
    moving = jnp.take(local, ordering, axis=1).reshape(draws, owners, per_pair)
    arrived = lax.all_to_all(moving, OWN, split_axis=1, concat_axis=1, tiled=True)
    spot_local = placings.reshape(-1) % points
    return jnp.zeros((draws, points), BF16).at[:, spot_local].set(arrived.reshape(draws, points))


def solution(mesh):
    return jax.shard_map(
        shards,
        mesh=mesh,
        in_specs=(
            P(None, ("groups", "blk", "sub"), "draw", None),
            P(None, ("groups", "blk", "sub"), None, None, None),
            P(None, ("groups", "blk", "sub"), None, None),
            P(("groups", "blk", "sub"), "draw", None),
            P(("groups", "blk", "sub"), "draw", None),
            P(None, ("groups", "blk", "sub"), None),
            P(("groups", "blk", "sub")),
        ),
        out_specs=P("draw", ("groups", "blk", "sub")),
        check_vma=False,
    )
```

```python
import functools

import jax
import jax.numpy as jnp
from jax import lax
from jax.experimental import pallas as pl
from jax.experimental.pallas import tpu as pltpu
from jax.sharding import PartitionSpec as P

K1 = 4
HALVES = 2
LANES = 128
OWN = ("blk", "sub")
MESH = pl.DeviceIdType.MESH
F32 = jnp.float32
BF16 = jnp.bfloat16


def repeat(count, body):
    if count <= 8:
        for at in range(count):
            body(at)
    else:
        pl.loop(0, count)(body)


def sweep(
    dims, regroup, neigh_hbm, spots_hbm, white_hbm, coup_hbm, diag_hbm, far, near, out,
    neigh, neigh_vm, spots, white, coup, diag, pool, flat, place, unplace, moved, landed,
    pos_out, pos_in, total, load_sem, push_send, push_recv, smem_sem, own_sem, prior_send,
    prior_recv, level_send, level_recv, pos_send, pos_recv, move_send, move_recv, stay_sem,
):
    blks, subs, levels, lb, draws, neighs = dims
    owners = blks * subs
    z, c = lax.axis_index("blk"), lax.axis_index("sub")
    me = z * subs + c
    mate = subs - 1 - c
    share_of = draws // subs
    half = share_of // HALVES
    chunks = levels * lb
    points = spots.shape[1] * LANES

    def device(owner):
        return {"blk": owner // subs, "sub": lax.rem(owner, subs)}

    def peer(step):
        return lax.rem(me + step, owners)

    def chip(step):
        return lax.rem(z + step, blks)

    def rows_of(core):
        return pl.ds(pl.multiple_of(core * share_of, share_of), share_of)

    wares = [(spots_hbm, spots.at[c]), (neigh_hbm, neigh_vm.at[c])]
    wares += [(coup_hbm.at[0], coup.at[c, 0]), (diag_hbm, diag.at[c])]
    wares += [(coup_hbm.at[i], coup.at[c, i]) for i in range(1, levels)]
    noise_at = len(wares)

    def load(i):
        src, dst = wares[i]
        return pltpu.make_async_copy(src, dst, load_sem.at[i])

    def push(i):
        src, dst = wares[i]
        return pltpu.make_async_remote_copy(
            src, dst, push_send.at[i], push_recv.at[i], device_id={"sub": mate}, device_id_type=MESH)

    def load_noise():
        return pltpu.make_async_copy(
            white_hbm.at[:, :, rows_of(c), :], white.at[c], load_sem.at[noise_at])

    def push_noise():
        return pltpu.make_async_remote_copy(
            white_hbm.at[:, :, rows_of(mate), :], white.at[c], push_send.at[noise_at],
            push_recv.at[noise_at], device_id={"sub": mate}, device_id_type=MESH)

    def ready(i):
        load(i).wait()
        push(i).wait_recv()

    priors = (far, near)

    def prior_rows(sec, h, core):
        return priors[sec].at[:, pl.ds(pl.multiple_of(core * share_of + h * half, half), half), :]

    def prior_slot(sec, h, owner):
        return pool[sec][h].at[pl.ds(owner * lb, lb)]

    def prior_stay(sec, h):
        return pltpu.make_async_copy(prior_rows(sec, h, c), prior_slot(sec, h, me), own_sem.at[sec, h])

    def prior_copy(sec, h, step, core):
        return pltpu.make_async_remote_copy(
            prior_rows(sec, h, core), prior_slot(sec, h, me), prior_send.at[sec, h, step, core],
            prior_recv.at[sec, h, me], device_id={"blk": chip(step), "sub": core}, device_id_type=MESH)

    def prior_across(sec, h):
        return pltpu.make_async_remote_copy(
            prior_rows(sec, h, mate), prior_slot(sec, h, me), prior_send.at[sec, h, 0, 0],
            prior_recv.at[sec, h, me], device_id={"sub": mate}, device_id_type=MESH)

    def prior_arrival(sec, h, owner):
        slot = prior_slot(sec, h, owner)
        return pltpu.make_async_remote_copy(
            slot, slot, prior_send.at[sec, h, 0, 0], prior_recv.at[sec, h, owner],
            device_id={"sub": mate}, device_id_type=MESH)

    def share_prior(sec, h):
        for core in range(subs):
            repeat(blks - 1, lambda i, core=core: prior_copy(sec, h, i + 1, core).start())
        prior_across(sec, h).start()

    def level_slot(sec, h, at):
        return pool[sec][h].at[pl.ds(at * (subs * lb), subs * lb)]

    def level_copy(sec, h, step):
        return pltpu.make_async_remote_copy(
            level_slot(sec, h, z), level_slot(sec, h, z), level_send.at[sec - 2, h, step],
            level_recv.at[sec - 2, h, z], device_id={"blk": chip(step), "sub": c}, device_id_type=MESH)

    def level_arrival(sec, h, at):
        return pltpu.make_async_remote_copy(
            level_slot(sec, h, at), level_slot(sec, h, at), level_send.at[sec - 2, h, 0],
            level_recv.at[sec - 2, h, at], device_id={"blk": chip(1), "sub": c}, device_id_type=MESH)

    def collect(sec, h):
        if sec < 2:
            prior_stay(sec, h).wait()
            repeat(owners - 1, lambda i: prior_arrival(sec, h, peer(i + 1)).wait_recv())
        else:
            repeat(blks - 1, lambda i: level_arrival(sec, h, chip(i + 1)).wait_recv())

    def pos_copy(step):
        to = peer(step)
        return pltpu.make_async_remote_copy(
            pos_out.at[to], pos_in.at[me], pos_send.at[step], pos_recv.at[me],
            device_id=device(to), device_id_type=MESH)

    def pos_arrival(owner):
        return pltpu.make_async_remote_copy(
            pos_out.at[owner], pos_in.at[owner], pos_send.at[0], pos_recv.at[owner],
            device_id=device(peer(1)), device_id_type=MESH)

    def landing(h, at, core):
        return landed.at[h, pl.ds(at * subs, subs), pl.ds(pl.multiple_of(core * half, half), half), :]

    def move_copy(h, step):
        to = peer(step)
        return pltpu.make_async_remote_copy(
            moved.at[h, to], landing(h, z, c), move_send.at[h, step], move_recv.at[h, me],
            device_id=device(to), device_id_type=MESH)

    def move_stay(h):
        return pltpu.make_async_copy(moved.at[h, me], landing(h, z, c), stay_sem.at[h])

    def move_arrival(h, at, core):
        owner = at * subs + core
        return pltpu.make_async_remote_copy(
            moved.at[h, owner], landing(h, at, core), move_send.at[h, 0], move_recv.at[h, owner],
            device_id=device(peer(1)), device_id_type=MESH)

    def lane():
        return lax.broadcasted_iota(jnp.int32, (LANES, points), 1).astype(F32)

    def rank_points(owner, own):
        spot = spots[owner]
        rows = spot.astype(F32)
        cols = rows.T
        local = lax.rem(spot, points).astype(F32).T
        ordered = jnp.zeros((1, points), F32)
        for k in range(chunks):
            col = cols[:, k:k + 1]
            below = jnp.zeros((LANES, LANES), F32)
            for j in range(chunks):
                below += jnp.where(rows[j:j + 1, :] < col, 1.0, 0.0)
            rank = jnp.sum(below, axis=1, keepdims=True)
            hit = lane() == rank
            place[owner, k * LANES:(k + 1) * LANES, :] = jnp.where(hit, 1.0, 0.0).astype(BF16)
            if own:
                ordered += jnp.sum(jnp.where(hit, local[:, k:k + 1], 0.0), axis=0, keepdims=True)
        if own:
            for s in range(owners):
                pos_out[s] = jnp.broadcast_to(ordered[:, s * LANES:(s + 1) * LANES], (8, LANES))
            pos_in[me] = pos_out[me]

    def place_arrivals():
        for i in range(1, owners):
            pos_arrival(peer(i)).wait_recv()
        for o in range(owners):
            col = pos_in[o].T[:, 0:1]
            unplace[o * LANES:(o + 1) * LANES, :] = jnp.where(lane() == col, 1.0, 0.0).astype(BF16)

    barrier = pltpu.get_barrier_semaphore()
    repeat(owners - 1, lambda i: pl.semaphore_signal(
        barrier, inc=1, device_id=device(peer(i + 1)), device_id_type=MESH))
    for i in range(2):
        load(i).start()
    for h in range(HALVES):
        for sec in (1, 0):
            prior_stay(sec, h).start()
    for i in range(2, noise_at):
        load(i).start()
    load_noise().start()
    load(0).wait()
    if regroup:
        rank_points(c, True)
    pl.semaphore_wait(barrier, owners - 1)
    for sec in (1, 0):
        share_prior(sec, 0)
    for i in range(4):
        push(i).start()
    push_noise().start()
    for h in range(1, HALVES):
        for sec in (1, 0):
            share_prior(sec, h)
    for i in range(4, noise_at):
        push(i).start()
    if regroup:
        for i in range(1, owners):
            pos_copy(i).start()
    push(0).wait_recv()
    if regroup:
        rank_points(mate, False)
    ready(1)
    to_smem = pltpu.make_async_copy(neigh_vm, neigh, smem_sem.at[0])
    to_smem.start()
    to_smem.wait()
    load_noise().wait()
    push_noise().wait_recv()
    for i in (2, 3):
        ready(i)

    def tiles(level, o, b, h, sec, first, last):
        rows = jnp.concatenate([pool[sec][h][neigh[o, level, b, k]] for k in range(first, last)], axis=1)
        factor = coup[o, level, b, first:last].reshape((last - first) * LANES, LANES)
        return jnp.dot(rows, factor, preferred_element_type=F32)

    def placed(level, o, span):
        rows = jnp.concatenate([flat[o, level * lb + b, span, :] for b in range(lb)], axis=1)
        width = lb * LANES
        return jnp.dot(rows, place[o, level * width:(level + 1) * width, :], preferred_element_type=F32)

    blocks = [(o, b) for o in range(subs) for b in range(lb)]
    for level in range(levels):
        if level > 0:
            ready(level + 3)
        for h in range(HALVES):
            span = slice(h * half, (h + 1) * half)
            if level == 0:
                collect(0, h)
            rest = [
                white[o, level, b, span, :] - tiles(level, o, b, h, level, K1, neighs)
                for o, b in blocks
            ]
            collect(level + 1, h)
            remain = [
                (r - tiles(level, o, b, h, level + 1, 0, K1)).astype(BF16)
                for r, (o, b) in zip(rest, blocks)
            ]
            for r, (o, b) in zip(remain, blocks):
                solved = jnp.dot(r, diag[o, level, b], preferred_element_type=F32).astype(BF16)
                flat[o, level * lb + b, span, :] = solved
                if level + 1 < levels:
                    pool[level + 2][h][z * (subs * lb) + o * lb + b] = solved
            if level + 1 < levels:
                repeat(blks - 1, lambda i: level_copy(level + 2, h, i + 1).start())
            elif regroup:
                for o in range(subs):
                    final = (total[o, span, :] + placed(level, o, span)).astype(BF16)
                    for s in range(owners):
                        moved[h, s, o] = final[:, s * LANES:(s + 1) * LANES]
                for i in range(1, owners):
                    move_copy(h, i).start()
                move_stay(h).start()
        if regroup and level + 1 < levels:
            for o in range(subs):
                part = placed(level, o, slice(0, share_of))
                total[o] = part if level == 0 else total[o] + part
            if level == 0:
                place_arrivals()

    if regroup:
        def laid(h, at):
            rows = jnp.concatenate([landed[h, at * subs + o] for o in range(subs)], axis=1)
            width = subs * LANES
            return jnp.dot(rows, unplace[pl.ds(pl.multiple_of(at * width, width), width), :],
                           preferred_element_type=F32)

        for h in range(HALVES):
            move_stay(h).wait()
            move_arrival(h, z, mate).wait_recv()
            whole = laid(h, z)
            for i in range(1, blks):
                for core in range(subs):
                    move_arrival(h, chip(i), core).wait_recv()
                whole += laid(h, chip(i))
            for core in range(subs):
                at = core * share_of + h * half
                out[at:at + half, :] = whole[core * half:(core + 1) * half].astype(BF16)
        for i in range(1, owners):
            pos_copy(i).wait_send()
            for h in range(HALVES):
                move_copy(h, i).wait_send()
    else:
        out[...] = flat[...]
    for h in range(HALVES):
        for sec in range(2):
            for core in range(subs):
                repeat(blks - 1, lambda i: prior_copy(sec, h, i + 1, core).wait_send())
            prior_across(sec, h).wait_send()
        for sec in range(2, levels + 1):
            repeat(blks - 1, lambda i: level_copy(sec, h, i + 1).wait_send())
    for i in range(noise_at):
        push(i).wait_send()
    push_noise().wait_send()


def shards(white_noise, coupling, diag_inv, prior_far, prior_near, neighbours, spot_map):
    blks, subs = lax.axis_size("blk"), lax.axis_size("sub")
    owners = blks * subs
    levels, lb, draws, size = white_noise.shape
    points = spot_map.shape[0]
    per_pair = points // owners
    regroup = per_pair == LANES
    chunks = levels * lb
    secs = levels + 1
    dims = (blks, subs, levels, lb, draws, neighbours.shape[2])
    share_of = draws // subs
    half = share_of // HALVES
    out_shape = (draws, points) if regroup else (subs, chunks, share_of, size)
    dma = pltpu.SemaphoreType.DMA
    vmem = pl.BlockSpec(memory_space=pltpu.VMEM)
    hbm = pl.BlockSpec(memory_space=pltpu.HBM)
    pairs = owners if regroup else 1
    flops = 2 * draws * size * size * chunks * 7 + 4 * draws * points * points
    result = pl.pallas_call(
        functools.partial(sweep, dims, regroup),
        out_shape=pltpu.VMEM(out_shape, BF16),
        in_specs=[hbm] * 7,
        out_specs=vmem,
        scratch_shapes=[
            pltpu.SMEM((subs, *neighbours.shape), jnp.int32),
            pltpu.VMEM((subs, *neighbours.shape), jnp.int32),
            pltpu.VMEM((subs, points // LANES, LANES), jnp.int32),
            pltpu.VMEM((subs, levels, lb, share_of, size), F32),
            pltpu.VMEM((subs, *coupling.shape), BF16),
            pltpu.VMEM((subs, *diag_inv.shape), BF16),
            [[pltpu.VMEM((owners * lb, half, size), BF16)] * HALVES] * secs,
            pltpu.VMEM((subs, chunks, share_of, size), BF16),
            pltpu.VMEM((subs, points, points), BF16),
            pltpu.VMEM((points, points), BF16),
            pltpu.VMEM((HALVES, pairs, subs, half, LANES), BF16),
            pltpu.VMEM((HALVES, pairs, subs * half, LANES), BF16),
            pltpu.VMEM((pairs, 8, LANES), F32),
            pltpu.VMEM((pairs, 8, LANES), F32),
            pltpu.VMEM((subs, share_of, points), F32),
            dma((levels + 4,)),
            dma((levels + 4,)),
            dma((levels + 4,)),
            dma((1,)),
            dma((2, HALVES)),
            dma((2, HALVES, blks, subs)),
            dma((2, HALVES, owners)),
            dma((levels - 1, HALVES, blks)),
            dma((levels - 1, HALVES, blks)),
            dma((owners,)),
            dma((owners,)),
            dma((HALVES, owners)),
            dma((HALVES, owners)),
            dma((HALVES,)),
        ],
        compiler_params=pltpu.CompilerParams(
            collective_id=0, has_side_effects=True, vmem_limit_bytes=60 * 1024 * 1024),
        cost_estimate=pl.CostEstimate(flops=flops, bytes_accessed=3 * 2**20, transcendentals=0),
    )(neighbours, spot_map.reshape(points // LANES, LANES), white_noise, coupling, diag_inv,
      prior_far, prior_near)
    if regroup:
        return result
    ordering = jnp.argsort(spot_map)
    sorted_spots = jnp.take(spot_map, ordering).reshape(owners, per_pair)
    placings = lax.all_to_all(sorted_spots, OWN, split_axis=0, concat_axis=0, tiled=True)
    result = lax.all_to_all(result, "sub", split_axis=0, concat_axis=2, tiled=True)[0]
    local = result.transpose(1, 0, 2).reshape(draws, points)
    moving = jnp.take(local, ordering, axis=1).reshape(draws, owners, per_pair)
    arrived = lax.all_to_all(moving, OWN, split_axis=1, concat_axis=1, tiled=True)
    spot_local = placings.reshape(-1) % points
    return jnp.zeros((draws, points), BF16).at[:, spot_local].set(arrived.reshape(draws, points))


def solution(mesh):
    return jax.shard_map(
        shards,
        mesh=mesh,
        in_specs=(
            P(None, ("groups", "blk", "sub"), "draw", None),
            P(None, ("groups", "blk", "sub"), None, None, None),
            P(None, ("groups", "blk", "sub"), None, None),
            P(("groups", "blk", "sub"), "draw", None),
            P(("groups", "blk", "sub"), "draw", None),
            P(None, ("groups", "blk", "sub"), None),
            P(("groups", "blk", "sub")),
        ),
        out_specs=P("draw", ("groups", "blk", "sub")),
        check_vma=False,
    )
```

```python
import functools

import jax
import jax.numpy as jnp
from jax import lax
from jax.experimental import pallas as pl
from jax.experimental.pallas import tpu as pltpu
from jax.sharding import PartitionSpec as P

K1 = 4
HALVES = 2
LANES = 128
OWN = ("blk", "sub")
MESH = pl.DeviceIdType.MESH
F32 = jnp.float32
BF16 = jnp.bfloat16


def repeat(count, body):
    if count <= 8:
        for at in range(count):
            body(at)
    else:
        pl.loop(0, count)(body)


def sweep(
    dims, regroup, neigh_hbm, spots_hbm, white_hbm, coup_hbm, diag_hbm, far, near, out,
    neigh, neigh_vm, spots, white, coup, diag, pool, flat, place, unplace, moved, landed,
    pos_out, pos_in, total, load_sem, push_send, push_recv, smem_sem, own_sem, prior_send,
    prior_recv, level_send, level_recv, pos_send, pos_recv, move_send, move_recv, stay_sem,
):
    blks, subs, levels, lb, draws, neighs = dims
    owners = blks * subs
    z, c = lax.axis_index("blk"), lax.axis_index("sub")
    me = z * subs + c
    mate = subs - 1 - c
    share_of = draws // subs
    half = share_of // HALVES
    chunks = levels * lb
    points = spots.shape[1] * LANES

    def device(owner):
        return {"blk": owner // subs, "sub": lax.rem(owner, subs)}

    def peer(step):
        return lax.rem(me + step, owners)

    def chip(step):
        return lax.rem(z + step, blks)

    def rows_of(core):
        return pl.ds(pl.multiple_of(core * share_of, share_of), share_of)

    wares = [(spots_hbm, spots.at[c]), (neigh_hbm, neigh_vm.at[c])]
    wares += [(coup_hbm.at[0], coup.at[c, 0]), (diag_hbm, diag.at[c])]
    wares += [(coup_hbm.at[i], coup.at[c, i]) for i in range(1, levels)]
    noise_at = len(wares)

    def load(i):
        src, dst = wares[i]
        return pltpu.make_async_copy(src, dst, load_sem.at[i])

    def push(i):
        src, dst = wares[i]
        return pltpu.make_async_remote_copy(
            src, dst, push_send.at[i], push_recv.at[i], device_id={"sub": mate}, device_id_type=MESH)

    def load_noise():
        return pltpu.make_async_copy(
            white_hbm.at[:, :, rows_of(c), :], white.at[c], load_sem.at[noise_at])

    def push_noise():
        return pltpu.make_async_remote_copy(
            white_hbm.at[:, :, rows_of(mate), :], white.at[c], push_send.at[noise_at],
            push_recv.at[noise_at], device_id={"sub": mate}, device_id_type=MESH)

    def ready(i):
        load(i).wait()
        push(i).wait_recv()

    priors = (far, near)

    def prior_rows(sec, h, core):
        return priors[sec].at[:, pl.ds(pl.multiple_of(core * share_of + h * half, half), half), :]

    def prior_slot(sec, h, owner):
        return pool[sec][h].at[pl.ds(owner * lb, lb)]

    def prior_stay(sec, h):
        return pltpu.make_async_copy(prior_rows(sec, h, c), prior_slot(sec, h, me), own_sem.at[sec, h])

    def prior_copy(sec, h, step, core):
        return pltpu.make_async_remote_copy(
            prior_rows(sec, h, core), prior_slot(sec, h, me), prior_send.at[sec, h, step, core],
            prior_recv.at[sec, h, me], device_id={"blk": chip(step), "sub": core}, device_id_type=MESH)

    def prior_across(sec, h):
        return pltpu.make_async_remote_copy(
            prior_rows(sec, h, mate), prior_slot(sec, h, me), prior_send.at[sec, h, 0, 0],
            prior_recv.at[sec, h, me], device_id={"sub": mate}, device_id_type=MESH)

    def prior_arrival(sec, h, owner):
        slot = prior_slot(sec, h, owner)
        return pltpu.make_async_remote_copy(
            slot, slot, prior_send.at[sec, h, 0, 0], prior_recv.at[sec, h, owner],
            device_id={"sub": mate}, device_id_type=MESH)

    def share_prior(sec, h):
        for core in range(subs):
            repeat(blks - 1, lambda i, core=core: prior_copy(sec, h, i + 1, core).start())
        prior_across(sec, h).start()

    def level_slot(sec, h, at):
        return pool[sec][h].at[pl.ds(at * (subs * lb), subs * lb)]

    def level_copy(sec, h, step):
        return pltpu.make_async_remote_copy(
            level_slot(sec, h, z), level_slot(sec, h, z), level_send.at[sec - 2, h, step],
            level_recv.at[sec - 2, h, z], device_id={"blk": chip(step), "sub": c}, device_id_type=MESH)

    def level_arrival(sec, h, at):
        return pltpu.make_async_remote_copy(
            level_slot(sec, h, at), level_slot(sec, h, at), level_send.at[sec - 2, h, 0],
            level_recv.at[sec - 2, h, at], device_id={"blk": chip(1), "sub": c}, device_id_type=MESH)

    def collect(sec, h):
        if sec < 2:
            prior_stay(sec, h).wait()
            repeat(owners - 1, lambda i: prior_arrival(sec, h, peer(i + 1)).wait_recv())
        else:
            repeat(blks - 1, lambda i: level_arrival(sec, h, chip(i + 1)).wait_recv())

    def pos_copy(step):
        to = peer(step)
        return pltpu.make_async_remote_copy(
            pos_out.at[to], pos_in.at[me], pos_send.at[step], pos_recv.at[me],
            device_id=device(to), device_id_type=MESH)

    def pos_arrival(owner):
        return pltpu.make_async_remote_copy(
            pos_out.at[owner], pos_in.at[owner], pos_send.at[0], pos_recv.at[owner],
            device_id=device(peer(1)), device_id_type=MESH)

    def landing(h, at, core):
        return landed.at[h, pl.ds(at * subs, subs), pl.ds(pl.multiple_of(core * half, half), half), :]

    def move_copy(h, step):
        to = peer(step)
        return pltpu.make_async_remote_copy(
            moved.at[h, to], landing(h, z, c), move_send.at[h, step], move_recv.at[h, me],
            device_id=device(to), device_id_type=MESH)

    def move_stay(h):
        return pltpu.make_async_copy(moved.at[h, me], landing(h, z, c), stay_sem.at[h])

    def move_arrival(h, at, core):
        owner = at * subs + core
        return pltpu.make_async_remote_copy(
            moved.at[h, owner], landing(h, at, core), move_send.at[h, 0], move_recv.at[h, owner],
            device_id=device(peer(1)), device_id_type=MESH)

    def lane():
        return lax.broadcasted_iota(jnp.int32, (LANES, points), 1).astype(F32)

    def rank_points(owner, own):
        spot = spots[owner]
        rows = spot.astype(F32)
        cols = rows.T
        local = lax.rem(spot, points).astype(F32).T
        ordered = jnp.zeros((1, points), F32)
        for k in range(chunks):
            col = cols[:, k:k + 1]
            below = jnp.zeros((LANES, LANES), F32)
            for j in range(chunks):
                below += jnp.where(rows[j:j + 1, :] < col, 1.0, 0.0)
            rank = jnp.sum(below, axis=1, keepdims=True)
            hit = lane() == rank
            place[owner, k * LANES:(k + 1) * LANES, :] = jnp.where(hit, 1.0, 0.0).astype(BF16)
            if own:
                ordered += jnp.sum(jnp.where(hit, local[:, k:k + 1], 0.0), axis=0, keepdims=True)
        if own:
            for s in range(owners):
                pos_out[s] = jnp.broadcast_to(ordered[:, s * LANES:(s + 1) * LANES], (8, LANES))
            pos_in[me] = pos_out[me]

    def place_arrivals():
        for i in range(1, owners):
            pos_arrival(peer(i)).wait_recv()
        for o in range(owners):
            col = pos_in[o].T[:, 0:1]
            unplace[o * LANES:(o + 1) * LANES, :] = jnp.where(lane() == col, 1.0, 0.0).astype(BF16)

    barrier = pltpu.get_barrier_semaphore()
    repeat(owners - 1, lambda i: pl.semaphore_signal(
        barrier, inc=1, device_id=device(peer(i + 1)), device_id_type=MESH))
    for i in range(2):
        load(i).start()
    for h in range(HALVES):
        for sec in (1, 0):
            prior_stay(sec, h).start()
    for i in range(2, noise_at):
        load(i).start()
    load_noise().start()
    pl.semaphore_wait(barrier, owners - 1)
    for sec in (1, 0):
        share_prior(sec, 0)
    for i in range(4):
        push(i).start()
    push_noise().start()
    for h in range(1, HALVES):
        for sec in (1, 0):
            share_prior(sec, h)
    for i in range(4, noise_at):
        push(i).start()
    load(0).wait()
    if regroup:
        rank_points(c, True)
        for i in range(1, owners):
            pos_copy(i).start()
    push(0).wait_recv()
    ready(1)
    to_smem = pltpu.make_async_copy(neigh_vm, neigh, smem_sem.at[0])
    to_smem.start()
    to_smem.wait()
    load_noise().wait()
    push_noise().wait_recv()
    for i in (2, 3):
        ready(i)

    def tiles(level, o, b, h, sec, first, last):
        rows = jnp.concatenate([pool[sec][h][neigh[o, level, b, k]] for k in range(first, last)], axis=1)
        factor = coup[o, level, b, first:last].reshape((last - first) * LANES, LANES)
        return jnp.dot(rows, factor, preferred_element_type=F32)

    def placed(level, o, span):
        rows = jnp.concatenate([flat[o, level * lb + b, span, :] for b in range(lb)], axis=1)
        width = lb * LANES
        return jnp.dot(rows, place[o, level * width:(level + 1) * width, :], preferred_element_type=F32)

    blocks = [(o, b) for o in range(subs) for b in range(lb)]
    for level in range(levels):
        if level > 0:
            ready(level + 3)
        for h in range(HALVES):
            span = slice(h * half, (h + 1) * half)
            if level == 0:
                collect(0, h)
            rest = [
                white[o, level, b, span, :] - tiles(level, o, b, h, level, K1, neighs)
                for o, b in blocks
            ]
            collect(level + 1, h)
            remain = [
                (r - tiles(level, o, b, h, level + 1, 0, K1)).astype(BF16)
                for r, (o, b) in zip(rest, blocks)
            ]
            for r, (o, b) in zip(remain, blocks):
                solved = jnp.dot(r, diag[o, level, b], preferred_element_type=F32).astype(BF16)
                flat[o, level * lb + b, span, :] = solved
                if level + 1 < levels:
                    pool[level + 2][h][z * (subs * lb) + o * lb + b] = solved
            if level + 1 < levels:
                repeat(blks - 1, lambda i: level_copy(level + 2, h, i + 1).start())
            elif regroup:
                for o in range(subs):
                    final = (total[o, span, :] + placed(level, o, span)).astype(BF16)
                    for s in range(owners):
                        moved[h, s, o] = final[:, s * LANES:(s + 1) * LANES]
                for i in range(1, owners):
                    move_copy(h, i).start()
                move_stay(h).start()
        if regroup and level == 0:
            rank_points(mate, False)
        if regroup and level + 1 < levels:
            for o in range(subs):
                part = placed(level, o, slice(0, share_of))
                total[o] = part if level == 0 else total[o] + part
            if level == 1:
                place_arrivals()

    if regroup:
        def laid(h, at):
            rows = jnp.concatenate([landed[h, at * subs + o] for o in range(subs)], axis=1)
            width = subs * LANES
            return jnp.dot(rows, unplace[pl.ds(pl.multiple_of(at * width, width), width), :],
                           preferred_element_type=F32)

        for h in range(HALVES):
            move_stay(h).wait()
            move_arrival(h, z, mate).wait_recv()
            whole = laid(h, z)
            for i in range(1, blks):
                for core in range(subs):
                    move_arrival(h, chip(i), core).wait_recv()
                whole += laid(h, chip(i))
            for core in range(subs):
                at = core * share_of + h * half
                out[at:at + half, :] = whole[core * half:(core + 1) * half].astype(BF16)
        for i in range(1, owners):
            pos_copy(i).wait_send()
            for h in range(HALVES):
                move_copy(h, i).wait_send()
    else:
        out[...] = flat[...]
    for h in range(HALVES):
        for sec in range(2):
            for core in range(subs):
                repeat(blks - 1, lambda i: prior_copy(sec, h, i + 1, core).wait_send())
            prior_across(sec, h).wait_send()
        for sec in range(2, levels + 1):
            repeat(blks - 1, lambda i: level_copy(sec, h, i + 1).wait_send())
    for i in range(noise_at):
        push(i).wait_send()
    push_noise().wait_send()


def shards(white_noise, coupling, diag_inv, prior_far, prior_near, neighbours, spot_map):
    blks, subs = lax.axis_size("blk"), lax.axis_size("sub")
    owners = blks * subs
    levels, lb, draws, size = white_noise.shape
    points = spot_map.shape[0]
    per_pair = points // owners
    regroup = per_pair == LANES
    chunks = levels * lb
    secs = levels + 1
    dims = (blks, subs, levels, lb, draws, neighbours.shape[2])
    share_of = draws // subs
    half = share_of // HALVES
    out_shape = (draws, points) if regroup else (subs, chunks, share_of, size)
    dma = pltpu.SemaphoreType.DMA
    vmem = pl.BlockSpec(memory_space=pltpu.VMEM)
    hbm = pl.BlockSpec(memory_space=pltpu.HBM)
    pairs = owners if regroup else 1
    flops = 2 * draws * size * size * chunks * 7 + 4 * draws * points * points
    result = pl.pallas_call(
        functools.partial(sweep, dims, regroup),
        out_shape=pltpu.VMEM(out_shape, BF16),
        in_specs=[hbm] * 7,
        out_specs=vmem,
        scratch_shapes=[
            pltpu.SMEM((subs, *neighbours.shape), jnp.int32),
            pltpu.VMEM((subs, *neighbours.shape), jnp.int32),
            pltpu.VMEM((subs, points // LANES, LANES), jnp.int32),
            pltpu.VMEM((subs, levels, lb, share_of, size), F32),
            pltpu.VMEM((subs, *coupling.shape), BF16),
            pltpu.VMEM((subs, *diag_inv.shape), BF16),
            [[pltpu.VMEM((owners * lb, half, size), BF16)] * HALVES] * secs,
            pltpu.VMEM((subs, chunks, share_of, size), BF16),
            pltpu.VMEM((subs, points, points), BF16),
            pltpu.VMEM((points, points), BF16),
            pltpu.VMEM((HALVES, pairs, subs, half, LANES), BF16),
            pltpu.VMEM((HALVES, pairs, subs * half, LANES), BF16),
            pltpu.VMEM((pairs, 8, LANES), F32),
            pltpu.VMEM((pairs, 8, LANES), F32),
            pltpu.VMEM((subs, share_of, points), F32),
            dma((levels + 4,)),
            dma((levels + 4,)),
            dma((levels + 4,)),
            dma((1,)),
            dma((2, HALVES)),
            dma((2, HALVES, blks, subs)),
            dma((2, HALVES, owners)),
            dma((levels - 1, HALVES, blks)),
            dma((levels - 1, HALVES, blks)),
            dma((owners,)),
            dma((owners,)),
            dma((HALVES, owners)),
            dma((HALVES, owners)),
            dma((HALVES,)),
        ],
        compiler_params=pltpu.CompilerParams(
            collective_id=0, has_side_effects=True, vmem_limit_bytes=60 * 1024 * 1024),
        cost_estimate=pl.CostEstimate(flops=flops, bytes_accessed=3 * 2**20, transcendentals=0),
    )(neighbours, spot_map.reshape(points // LANES, LANES), white_noise, coupling, diag_inv,
      prior_far, prior_near)
    if regroup:
        return result
    ordering = jnp.argsort(spot_map)
    sorted_spots = jnp.take(spot_map, ordering).reshape(owners, per_pair)
    placings = lax.all_to_all(sorted_spots, OWN, split_axis=0, concat_axis=0, tiled=True)
    result = lax.all_to_all(result, "sub", split_axis=0, concat_axis=2, tiled=True)[0]
    local = result.transpose(1, 0, 2).reshape(draws, points)
    moving = jnp.take(local, ordering, axis=1).reshape(draws, owners, per_pair)
    arrived = lax.all_to_all(moving, OWN, split_axis=1, concat_axis=1, tiled=True)
    spot_local = placings.reshape(-1) % points
    return jnp.zeros((draws, points), BF16).at[:, spot_local].set(arrived.reshape(draws, points))


def solution(mesh):
    return jax.shard_map(
        shards,
        mesh=mesh,
        in_specs=(
            P(None, ("groups", "blk", "sub"), "draw", None),
            P(None, ("groups", "blk", "sub"), None, None, None),
            P(None, ("groups", "blk", "sub"), None, None),
            P(("groups", "blk", "sub"), "draw", None),
            P(("groups", "blk", "sub"), "draw", None),
            P(None, ("groups", "blk", "sub"), None),
            P(("groups", "blk", "sub")),
        ),
        out_specs=P("draw", ("groups", "blk", "sub")),
        check_vma=False,
    )
```
